32 devices in a mesh: group: 2 (over y), ep: 4 (over x, core), side: 4 (over z).
Axes of the slice: x: 2, y: 2, z: 4, core: 2. Of those that a mesh axis runs over, the one named last changes fastest.
Arguments:
- queries: bfloat16 [64, 128, 576], P(('group', 'ep', 'side')), parts along dimension 0, may hold values from -6 to 6
- cache: bfloat16 [64, 256, 576], P(('group', 'ep', 'side')), parts along dimension 0, may hold values from -6 to 6
- lengths: int32 [64], P(('group', 'ep', 'side')), parts along dimension 0, may hold values from 2 to 256, as said below
- resid: bfloat16 [64, 7168], P(('group', 'ep', 'side')), parts along dimension 0, may hold values from -6 to 6
- uv_weight: bfloat16 [128, 512, 128], P(('ep', 'side')), may hold values from -0.25 to 0.25
- out_weight: bfloat16 [16384, 7168], P(('ep', 'side')), may hold values from -0.046875 to 0.046875
- norm_gain: bfloat16 [7168], replicated, may hold values from 0.5 to 1.5
- expert_ids: int32 [64, 2], P(('group', 'ep', 'side')), parts along dimension 0, may hold values from 0 to 3, all different within a row; in each aligned block of 2 rows (0 to 1, 2 to 3, ...) at most 2 rows name the same one
- route_weights: float32 [64, 2], P(('group', 'ep', 'side')), parts along dimension 0, may hold values from 0.1 to 1
- gate_weight: bfloat16 [4, 7168, 2048], P('ep', None, 'side'), may hold values from -0.0625 to 0.0625
- up_weight: bfloat16 [4, 7168, 2048], P('ep', None, 'side'), may hold values from -0.0625 to 0.0625
- down_weight: bfloat16 [4, 2048, 7168], P('ep', 'side'), may hold values from -0.125 to 0.125
Outputs:
- layer_out: bfloat16 [64, 7168], P(('group', 'ep', 'side')), parts along dimension 0
The draws below stay inside these ranges and needn't reach their ends.
There are 2 independent parts, one for each index of `group`. The reference program is written for one: setup_inputs(seed, part) draws one part's arguments, and reference() takes and returns one part's arrays. A program takes and returns all parts, laid end to end along the dimension named above; an argument that names none is the same for every part. Nothing has to cross between parts.
Inputs may be any that keep to these rules, and one draw needn't show every extreme that they name: `lengths`: the used slots of a row are its first ones; some row uses all 256. `expert_ids`: each row names 2 different experts.
All inputs are finite; a program needn't handle non-finite values.
Results may differ from the reference program's by a relative error of at most 0.0075.
Values may be sent and summed in bfloat16 or wider, within the bound.
A program may use at most 128 MiB of HBM per device.

```python
import math
import jax
import jax.numpy as jnp
import numpy as np
from jax import lax

D = 7168
FF = 2048
HEADS = 128
HEAD_DIM = 128
LATENT = 512
ROPE = 64
ROWS_DEV = 2
L = 256
ROWS = 32
EXPERTS = 4
TOP = 2
CAP = 2


def lengths_from(key):
    drawn_lengths = jax.random.randint(key, (ROWS,), 2, L + 1).astype(jnp.int32)
    return drawn_lengths.at[0].set(L).at[1].set(2)


def draw_lengths(key, part):
    key = jax.random.fold_in(key, 7)
    return lengths_from(key)


def draw_queries(key, part):
    key = jax.random.fold_in(key, 3)
    array_shape = (ROWS, HEADS, LATENT + ROPE)
    values = jax.random.truncated_normal(key, -6.0, 6.0, array_shape, jnp.float32)
    return values.astype(jnp.bfloat16)


def draw_cache(key, part):
    key = jax.random.fold_in(key, 5)
    components = LATENT + ROPE
    array_shape = (ROWS, L, components)
    values = jax.random.truncated_normal(key, -6.0, 6.0, array_shape, jnp.float32)
    return values.astype(jnp.bfloat16)


def block_levels(rng, extent, cuts, smallest, largest):
    def one(position, blocks):
        heights = jax.random.uniform(jax.random.fold_in(jax.random.fold_in(rng, 6), position), (blocks,), jnp.float32, smallest / len(cuts), largest / len(cuts))
        return jnp.repeat(jnp.exp(heights), extent[position] // blocks).reshape((-1,) + (1,) * (len(extent) - position - 1))

    factor_of = one(*cuts[0])
    for cut in cuts[1:]:
        factor_of = factor_of * one(*cut)
    return factor_of


def assign_block(stream_key, own, number, rows, count, top, reach, lean):
    order = jax.random.permutation(stream_key, count)
    packed, common = portions_of(count, rows * top, reach, lean, True), portions_of(count, rows * top, reach, lean, False)
    places = jnp.arange(count)

    def named(sizes, turn):
        used = int((sizes > 0).sum())
        fixed = max(1, used // 4)
        moved = fixed + (places - fixed + turn * (used - fixed)) % max(1, count - fixed)
        return jnp.zeros((count,), jnp.int32).at[order[jnp.where(places < fixed, places, moved)]].set(jnp.asarray(sizes, jnp.int32))

    sizes = jnp.where(number % 4 == 0, named(packed, number // 4), named(common, number - number // 4 - 1))
    mixed = jax.random.permutation(jax.random.fold_in(own, 3), count)
    giver, receiver = mixed[0:count // 2 * 2:2], mixed[1:count // 2 * 2:2]
    room = jnp.minimum(sizes[giver] - 1, reach - sizes[receiver]) // 2
    room = jnp.where((giver == order[0]) | (receiver == order[0]) | (sizes[receiver] == 0), 0, jnp.maximum(room, 0))
    moved = jax.random.randint(jax.random.fold_in(own, 4), (count // 2,), 0, 1 << 20) % (room + 1)
    sizes = sizes.at[giver].add(-moved).at[receiver].add(moved)
    labels = jnp.searchsorted(jnp.cumsum(sizes), jnp.arange(rows * top), side="right").astype(jnp.int32)
    listing = labels.reshape(top, rows).T
    listing = listing[jax.random.permutation(jax.random.fold_in(own, 1), rows)]
    turn = jax.random.randint(jax.random.fold_in(own, 2), (rows, 1), 0, top)
    return jnp.take_along_axis(listing, (jnp.arange(top)[None, :] + turn) % top, axis=1)


def portions_of(count, total, most, lean, full):
    portions = [(1 << 20) // math.isqrt(grade ** lean) + 1 for grade in range(1, count + 1)]
    largest = most if full else min(most, max(-(-total // count), total * portions[0] // sum(portions)))
    least = 1 if total - largest >= count - 1 else 0
    given, spare = [largest] + [least] * (count - 1), total - largest - least * (count - 1)
    while spare > 0:
        candidates = [i for i in range(1, count) if given[i] < largest] or [i for i in range(1, count) if given[i] < most]
        mass, left = sum([portions[i] for i in candidates]), spare
        for i in candidates:
            extra = min(most - given[i], max(1, left * portions[i] // mass), spare)
            given[i] = given[i] + extra
            spare = spare - extra
    return np.array(given)


def centred(own_key, dims, scale, most, cuts=(), kind=jnp.bfloat16):
    result = jax.random.normal(own_key, dims, jnp.float32) * scale
    if len(cuts) > 0:
        result = block_levels(own_key, dims, cuts, -0.22, 0.18) * result
    return jnp.clip(result, min=-most, max=most).astype(kind)


def setup_inputs(seed: int = 0, part: int = 0) -> dict:
    streams_of = jax.random.split(jax.random.key(seed), 13)
    part_keys = jax.random.split(jax.random.fold_in(streams_of[12], part), 13)
    queries = draw_queries(jax.random.fold_in(jax.random.fold_in(streams_of[12], part), 71), part)
    cache = draw_cache(jax.random.fold_in(jax.random.fold_in(streams_of[12], part), 71), part)
    lengths = draw_lengths(jax.random.fold_in(jax.random.fold_in(streams_of[12], part), 71), part)
    resid = centred(part_keys[3], (ROWS, D), 1.0, 6.0, ((0, 16),))
    uv_weight = centred(streams_of[4], (HEADS, LATENT, HEAD_DIM), LATENT ** -0.5, 0.25, ((0, 16),))
    out_weight = centred(streams_of[5], (HEADS * HEAD_DIM, D), (HEADS * HEAD_DIM) ** -0.5, 0.046875, ((0, 16),))
    norm_gain = jnp.clip(1.0 + 0.1 * jax.random.normal(streams_of[6], (D,), jnp.float32), 0.5, 1.5).astype(jnp.bfloat16)
    expert_ids_keys = jax.random.split(jax.random.fold_in(part_keys[7], 1), ROWS // ROWS_DEV)
    expert_ids_turns = jax.random.permutation(jax.random.fold_in(part_keys[7], 3), ROWS // ROWS_DEV)
    expert_ids = jax.vmap(lambda own, number: assign_block(jax.random.fold_in(part_keys[7], 2), own, number, ROWS_DEV, EXPERTS, TOP, CAP, 2))(expert_ids_keys, expert_ids_turns).reshape((ROWS, TOP))
    route_weights = jnp.clip(0.1 + 0.9 * jax.random.uniform(part_keys[8], (ROWS, TOP), jnp.float32) ** block_levels(part_keys[8], (ROWS, TOP), ((0, 16),), -0.2, 0.2), 0.1, 1.0)
    gate_weight = centred(streams_of[9], (EXPERTS, D, FF), D ** -0.5, 0.0625, ((0, 4), (2, 4)))
    up_weight = centred(streams_of[10], (EXPERTS, D, FF), D ** -0.5, 0.0625, ((0, 4), (2, 4)))
    down_weight = centred(streams_of[11], (EXPERTS, FF, D), FF ** -0.5, 0.125, ((0, 4), (1, 4)))
    return dict(queries=queries, cache=cache, lengths=lengths, resid=resid, uv_weight=uv_weight, out_weight=out_weight, norm_gain=norm_gain, expert_ids=expert_ids, route_weights=route_weights, gate_weight=gate_weight, up_weight=up_weight, down_weight=down_weight)


def reference(queries, cache, lengths, resid, uv_weight, out_weight, norm_gain, expert_ids, route_weights, gate_weight, up_weight, down_weight):
    scale = 1.0 / 192.0 ** 0.5
    scores = jnp.einsum('rhk,rtk->rht', queries.astype(jnp.float32), cache.astype(jnp.float32)) * scale
    slots = jnp.arange(L, dtype=jnp.int32)
    valid = slots[None, None, :] < lengths[:, None, None]
    top_score = lax.optimization_barrier(jnp.max(jnp.where(valid, scores, -1e+30), axis=2, keepdims=True))
    expo = jnp.where(valid, jnp.exp(scores - top_score), 0.0)
    probs = (expo / lax.optimization_barrier(jnp.sum(expo, axis=2, keepdims=True))).astype(jnp.bfloat16)
    context = jnp.einsum('rht,rtc->rhc', probs.astype(jnp.float32), cache[:, :, :LATENT].astype(jnp.float32)).astype(jnp.bfloat16)
    values = jnp.einsum('rhc,hcd->rhd', context.astype(jnp.float32), uv_weight.astype(jnp.float32)).astype(jnp.bfloat16)
    attn = jnp.dot(values.reshape(ROWS, HEADS * HEAD_DIM), out_weight, preferred_element_type=jnp.float32)
    hidden_state = (resid.astype(jnp.float32) + attn).astype(jnp.bfloat16)
    wide = hidden_state.astype(jnp.float32)
    normed = (wide * lax.rsqrt(lax.optimization_barrier(jnp.mean(wide * wide, axis=1, keepdims=True)) + 1e-06) * norm_gain.astype(jnp.float32)).astype(jnp.bfloat16)
    experts_range = jnp.arange(EXPERTS, dtype=jnp.int32)
    coef = lax.optimization_barrier(jnp.sum(route_weights[:, :, None] * (expert_ids[:, :, None] == experts_range[None, None, :]).astype(jnp.float32), axis=1))

    def one_expert(operands):
        gate_w, up_w, down_w = operands
        gate = jnp.dot(normed, gate_w, preferred_element_type=jnp.float32)
        upper = jnp.dot(normed, up_w, preferred_element_type=jnp.float32)
        inner = (jax.nn.silu(gate) * upper).astype(jnp.bfloat16)
        return jnp.dot(inner, down_w, preferred_element_type=jnp.float32).astype(jnp.bfloat16)
    expert_out = lax.map(one_expert, (gate_weight, up_weight, down_weight))
    mixed = jnp.einsum('re,erd->rd', coef, expert_out.astype(jnp.float32))
    return (wide + mixed).astype(jnp.bfloat16)
```

```python
import functools

import jax
import jax.numpy as jnp
from jax import lax
from jax.experimental import pallas as pl
from jax.experimental.pallas import tpu as pltpu
from jax.sharding import PartitionSpec as P

F32 = jnp.float32
BF16 = jnp.bfloat16
MESH = pl.DeviceIdType.MESH
CHUNKS = 4


def layer_kernel(
    ep_n,
    side_n,
    lengths,
    ids,
    route,
    q_hbm,
    cache_hbm,
    resid,
    gain,
    uv_hbm,
    ow_hbm,
    gw_hbm,
    uw_hbm,
    dw_hbm,
    out,
    q,
    cache,
    uv,
    ow,
    gw,
    uw,
    dw,
    ctx_tx,
    ctx_rx,
    ctx_rows,
    vals,
    cf_tx,
    cf_rx,
    cf_rows,
    part,
    t1,
    r1,
    t2,
    r2,
    t3,
    r3,
    keep,
    hidden,
    gath,
    xrows,
    in_sem,
    ow_sem,
    gw_sem,
    uw_sem,
    dw_sem,
    ctx_send,
    ctx_recv,
    cf_send,
    cf_recv,
    rs_send,
    rs_recv,
    ag_send,
    ag_recv,
):
    n = ep_n * side_n
    x_n = ep_n // 2
    ep = lax.axis_index("ep")
    side = lax.axis_index("side")
    me = ep * side_n + side
    x = ep // 2
    core = lax.rem(ep, 2)
    rows_here, heads, _ = q_hbm.shape
    heads_here, latent, value_size = uv_hbm.shape
    slots = cache_hbm.shape[1]
    width = resid.shape[1]
    piece = width // CHUNKS
    rows = n * rows_here
    block = side_n * rows_here

    def at(group_index):
        return {"ep": group_index // side_n, "side": lax.rem(group_index, side_n)}

    def remote(src, dst, send, recv, device):
        return pltpu.make_async_remote_copy(
            src_ref=src, dst_ref=dst, send_sem=send, recv_sem=recv, device_id=device, device_id_type=MESH
        )

    barrier = pltpu.get_barrier_semaphore()

    @pl.loop(1, n)
    def _(i):
        pl.semaphore_signal(barrier, inc=1, device_id=at(lax.rem(me + i, n)), device_id_type=MESH)

    loads = [
        pltpu.make_async_copy(cache_hbm, cache, in_sem.at[0]),
        pltpu.make_async_copy(q_hbm, q, in_sem.at[1]),
        pltpu.make_async_copy(uv_hbm, uv, in_sem.at[2]),
    ]
    for load in loads:
        load.start()
    cut = [pl.ds(c * piece, piece) for c in range(CHUNKS)]
    ow_load = [pltpu.make_async_copy(ow_hbm.at[:, s], ow.at[:, s], ow_sem.at[c]) for c, s in enumerate(cut)]
    gw_load = [pltpu.make_async_copy(gw_hbm.at[0, s], gw.at[s], gw_sem.at[c]) for c, s in enumerate(cut)]
    uw_load = [pltpu.make_async_copy(uw_hbm.at[0, s], uw.at[s], uw_sem.at[c]) for c, s in enumerate(cut)]
    dw_load = [pltpu.make_async_copy(dw_hbm.at[0, :, s], dw.at[:, s], dw_sem.at[c]) for c, s in enumerate(cut)]
    for load in ow_load:
        load.start()
    for c in range(CHUNKS):
        gw_load[c].start()
        uw_load[c].start()
    for load in dw_load:
        load.start()

    lane = lax.broadcasted_iota(jnp.int32, (1, 128), 1)
    for r in range(rows_here):
        line = jnp.zeros((1, 128), F32)
        for k in range(ids.shape[1]):
            line += jnp.where(lane == ids[r, k], route[r, k], 0.0)
        cf_tx[r : r + 1, :] = line
    cf_rx[me] = cf_tx[...]

    def attend(r):
        scores = lax.dot_general(
            q[r], cache[r], (((1,), (1,)), ((), ())), preferred_element_type=F32
        ) * (1.0 / 192.0**0.5)
        valid = lax.broadcasted_iota(jnp.int32, (heads, slots), 1) < lengths[r]
        top = jnp.max(jnp.where(valid, scores, -1e30), axis=1, keepdims=True)
        expo = jnp.where(valid, jnp.exp(scores - top), 0.0)
        probs = (expo / jnp.sum(expo, axis=1, keepdims=True)).astype(BF16)
        context = jnp.dot(probs, cache[r, :, :latent], preferred_element_type=F32)
        for d in range(n):
            ctx_tx[r, d] = context[d * heads_here : (d + 1) * heads_here].astype(BF16)
        ctx_rx[r, me] = ctx_tx[r, me]

    def send_context(r):
        @pl.loop(1, n)
        def _(i):
            there = lax.rem(me + i, n)
            remote(
                ctx_tx.at[r, there], ctx_rx.at[r, me], ctx_send.at[r, i - 1], ctx_recv.at[r, i - 1], at(there)
            ).start()

    loads[0].wait()
    loads[1].wait()
    for r in range(rows_here):
        attend(r)
        if r == 0:
            pl.semaphore_wait(barrier, n - 1)
        send_context(r)

    @pl.loop(1, n)
    def _(i):
        remote(cf_tx, cf_rx.at[me], cf_send.at[i - 1], cf_recv.at[i - 1], at(lax.rem(me + i, n))).start()

    loads[2].wait()
    for r in range(rows_here):

        @pl.loop(1, n)
        def _(i):
            origin = lax.rem(me + n - i, n)
            remote(
                ctx_tx.at[r, origin], ctx_rx.at[r, origin], ctx_send.at[r, i - 1], ctx_recv.at[r, i - 1], at(origin)
            ).wait_recv()

    for r in range(rows_here):
        for d in range(n):
            first = (d * rows_here + r) * heads_here
            arrived = ctx_rx[r, d].astype(F32)
            for j in range(latent // 128):
                ctx_rows[j, first : first + heads_here] = arrived[:, j * 128 : (j + 1) * 128]
    for h in range(heads_here):
        picked = pl.ds(h, rows, stride=heads_here) if heads_here > 1 else pl.ds(0, rows)
        taken = jnp.concatenate([ctx_rows[j, picked, :] for j in range(latent // 128)], axis=1)
        vals[:, h * value_size : (h + 1) * value_size] = jnp.dot(
            taken.astype(BF16), uv[h], preferred_element_type=F32
        ).astype(BF16)

    def reduce_copies(p, c):
        core_copy = remote(
            t1.at[p, c], r1.at[p, c], rs_send.at[p, c, 0], rs_recv.at[p, c, 0], {"ep": ep + 1 - 2 * core}
        )
        x_copies, side_copies = [], []
        for i in range(1, x_n):
            there = lax.rem(x + i, x_n) * 2 + core
            x_copies.append(
                remote(t2.at[p, c, i - 1], r2.at[p, c, i - 1], rs_send.at[p, c, i], rs_recv.at[p, c, i], {"ep": there})
            )
        for i in range(1, side_n):
            k = x_n + i - 1
            there = lax.rem(side + i, side_n)
            side_copies.append(
                remote(t3.at[p, c, there], r3.at[p, c, i - 1], rs_send.at[p, c, k], rs_recv.at[p, c, k], {"side": there})
            )
        return core_copy, x_copies, side_copies

    def reduce_scatter(p, product):
        copies = [reduce_copies(p, c) for c in range(CHUNKS)]
        totals = []
        for step in range(CHUNKS + 2):
            c = step
            if c < CHUNKS:
                part[c] = product(c).reshape(ep_n, block, piece)
                for k in range(x_n):
                    t1[p, c, k] = part[c, 2 * k + 1 - core].astype(BF16)
                copies[c][0].start()
            c = step - 1
            if 0 <= c < CHUNKS:
                copies[c][0].wait_recv()
                for i in range(1, x_n):
                    k = lax.rem(x + i, x_n)
                    t2[p, c, i - 1] = (part[c, 2 * k + core] + r1[p, c, k].astype(F32)).astype(BF16)
                    copies[c][1][i - 1].start()
            c = step - 2
            if 0 <= c < CHUNKS:
                total = part[c, ep] + r1[p, c, x].astype(F32)
                for i in range(1, x_n):
                    copies[c][1][i - 1].wait_recv()
                    total += r2[p, c, i - 1].astype(F32)
                for s in range(side_n):
                    mine = total[s * rows_here : (s + 1) * rows_here]
                    keep[c, s] = mine
                    t3[p, c, s] = mine.astype(BF16)
                for copy in copies[c][2]:
                    copy.start()
        for c in range(CHUNKS):
            total = keep[c, side]
            for i in range(1, side_n):
                copies[c][2][i - 1].wait_recv()
                total += r3[p, c, i - 1].astype(F32)
            totals.append(total)
        return totals, copies

    def out_product(c):
        ow_load[c].wait()
        return jnp.dot(vals[...], ow[:, cut[c]], preferred_element_type=F32)

    attn, copies_a = reduce_scatter(0, out_product)

    square = jnp.zeros((rows_here, 1), F32)
    for c in range(CHUNKS):
        state = (resid[:, cut[c]].astype(F32) + attn[c]).astype(BF16).astype(F32)
        hidden[:, cut[c]] = state
        square += jnp.sum(state * state, axis=1, keepdims=True)
    inverse = lax.rsqrt(square * (1.0 / width) + 1e-06)

    def gather_copies(c):
        def blocks(index):
            return gath.at[c, pl.ds(index * side_n, side_n)]

        side_out, side_in, x_out, x_in, core_out, core_in = [], [], [], [], [], []
        for i in range(1, side_n):
            k = i - 1
            origin = ep * side_n + lax.rem(side + side_n - i, side_n)
            there = {"side": lax.rem(side + i, side_n)}
            side_out.append(remote(gath.at[c, me], gath.at[c, me], ag_send.at[c, k], ag_recv.at[c, k], there))
            side_in.append(remote(gath.at[c, origin], gath.at[c, origin], ag_send.at[c, k], ag_recv.at[c, k], there))
        for i in range(1, x_n):
            k = side_n + i - 2
            origin = lax.rem(x + x_n - i, x_n) * 2 + core
            there = {"ep": lax.rem(x + i, x_n) * 2 + core}
            x_out.append(remote(blocks(ep), blocks(ep), ag_send.at[c, k], ag_recv.at[c, k], there))
            x_in.append(remote(blocks(origin), blocks(origin), ag_send.at[c, k], ag_recv.at[c, k], there))
        for i in range(x_n):
            k = side_n + x_n - 2 + i
            origin = lax.rem(x + x_n - i, x_n) * 2
            sibling = {"ep": ep + 1 - 2 * core}
            mine, other = blocks(origin + core), blocks(origin + 1 - core)
            core_out.append(remote(mine, mine, ag_send.at[c, k], ag_recv.at[c, k], sibling))
            core_in.append(remote(other, other, ag_send.at[c, k], ag_recv.at[c, k], sibling))
        return side_out, side_in, x_out, x_in, core_out, core_in

    gathers = [gather_copies(c) for c in range(CHUNKS)]
    for c in range(CHUNKS):
        gath[c, me] = (hidden[:, cut[c]] * inverse * gain[:, cut[c]].astype(F32)).astype(BF16)
        for copy in gathers[c][0]:
            copy.start()
    for c in range(CHUNKS):
        for copy in gathers[c][1]:
            copy.wait_recv()
        for copy in gathers[c][2]:
            copy.start()
        gathers[c][4][0].start()
    for c in range(CHUNKS):
        for i in range(1, x_n):
            gathers[c][3][i - 1].wait_recv()
            gathers[c][4][i].start()

    @pl.loop(1, n)
    def _(i):
        origin = lax.rem(me + n - i, n)
        remote(cf_tx, cf_rx.at[origin], cf_send.at[i - 1], cf_recv.at[i - 1], at(origin)).wait_recv()

    for d in range(n):
        cf_rows[d * rows_here : (d + 1) * rows_here] = cf_rx[d]
    coef = jnp.sum(jnp.where(lane == ep, cf_rows[...], 0.0), axis=1, keepdims=True)

    gate = jnp.zeros((rows, gw.shape[1]), F32)
    upper = jnp.zeros((rows, gw.shape[1]), F32)
    for c in range(CHUNKS):
        for copy in gathers[c][5]:
            copy.wait_recv()
        for d in range(n):
            xrows[c, d * rows_here : (d + 1) * rows_here] = gath[c, d].astype(F32)
        normed = xrows[c].astype(BF16)
        gw_load[c].wait()
        uw_load[c].wait()
        gate += jnp.dot(normed, gw[cut[c]], preferred_element_type=F32)
        upper += jnp.dot(normed, uw[cut[c]], preferred_element_type=F32)
    inner = (jax.nn.silu(gate) * upper * coef).astype(BF16)

    def down_product(c):
        dw_load[c].wait()
        return jnp.dot(inner, dw[:, cut[c]], preferred_element_type=F32)

    mixed, copies_b = reduce_scatter(1, down_product)
    for c in range(CHUNKS):
        out[:, cut[c]] = (hidden[:, cut[c]] + mixed[c]).astype(out.dtype)

    @pl.loop(1, n)
    def _(i):
        there = lax.rem(me + i, n)
        for r in range(rows_here):
            remote(
                ctx_tx.at[r, there], ctx_rx.at[r, me], ctx_send.at[r, i - 1], ctx_recv.at[r, i - 1], at(there)
            ).wait_send()
        remote(cf_tx, cf_rx.at[me], cf_send.at[i - 1], cf_recv.at[i - 1], at(there)).wait_send()

    for copies in (copies_a, copies_b):
        for core_copy, x_copies, side_copies in copies:
            for copy in [core_copy] + x_copies + side_copies:
                copy.wait_send()
    for side_out, _, x_out, _, core_out, _ in gathers:
        for copy in side_out + x_out + core_out:
            copy.wait_send()


def on_device(
    queries,
    cache,
    lengths,
    resid,
    uv_weight,
    out_weight,
    norm_gain,
    expert_ids,
    route_weights,
    gate_weight,
    up_weight,
    down_weight,
):
    ep_n = lax.axis_size("ep")
    side_n = lax.axis_size("side")
    n = ep_n * side_n
    x_n = ep_n // 2
    rows_here, _, _ = queries.shape
    heads_here, latent, value_size = uv_weight.shape
    width = resid.shape[1]
    piece = width // CHUNKS
    rows = n * rows_here
    block = side_n * rows_here
    vmem = pltpu.VMEM
    dma = pltpu.SemaphoreType.DMA
    hops = 1 + (x_n - 1) + (side_n - 1)
    gather_hops = (side_n - 1) + (x_n - 1) + x_n
    smem_spec = pl.BlockSpec(memory_space=pltpu.SMEM)
    vmem_spec = pl.BlockSpec(memory_space=pltpu.VMEM)
    any_spec = pl.BlockSpec(memory_space=pl.ANY)
    return pl.pallas_call(
        functools.partial(layer_kernel, ep_n, side_n),
        out_shape=jax.ShapeDtypeStruct(resid.shape, resid.dtype),
        in_specs=[smem_spec] * 3 + [any_spec] * 2 + [vmem_spec] * 2 + [any_spec] * 5,
        out_specs=vmem_spec,
        scratch_shapes=[
            vmem(queries.shape, BF16),
            vmem(cache.shape, BF16),
            vmem(uv_weight.shape, BF16),
            vmem(out_weight.shape, BF16),
            vmem(gate_weight.shape[1:], BF16),
            vmem(up_weight.shape[1:], BF16),
            vmem(down_weight.shape[1:], BF16),
            vmem((rows_here, n, heads_here, latent), BF16),
            vmem((rows_here, n, heads_here, latent), BF16),
            vmem((latent // 128, rows * heads_here, 128), F32),
            vmem((rows, heads_here * value_size), BF16),
            vmem((rows_here, 128), F32),
            vmem((n, rows_here, 128), F32),
            vmem((rows, 128), F32),
            vmem((CHUNKS, ep_n, block, piece), F32),
            vmem((2, CHUNKS, x_n, block, piece), BF16),
            vmem((2, CHUNKS, x_n, block, piece), BF16),
            vmem((2, CHUNKS, x_n - 1, block, piece), BF16),
            vmem((2, CHUNKS, x_n - 1, block, piece), BF16),
            vmem((2, CHUNKS, side_n, rows_here, piece), BF16),
            vmem((2, CHUNKS, side_n - 1, rows_here, piece), BF16),
            vmem((CHUNKS, side_n, rows_here, piece), F32),
            vmem((rows_here, width), F32),
            vmem((CHUNKS, n, rows_here, piece), BF16),
            vmem((CHUNKS, rows, piece), F32),
            dma((3,)),
            dma((CHUNKS,)),
            dma((CHUNKS,)),
            dma((CHUNKS,)),
            dma((CHUNKS,)),
            dma((rows_here, n - 1)),
            dma((rows_here, n - 1)),
            dma((n - 1,)),
            dma((n - 1,)),
            dma((2, CHUNKS, hops)),
            dma((2, CHUNKS, hops)),
            dma((CHUNKS, gather_hops)),
            dma((CHUNKS, gather_hops)),
        ],
        compiler_params=pltpu.CompilerParams(
            collective_id=0, has_side_effects=True, vmem_limit_bytes=56 * 2**20
        ),
    )(
        lengths,
        expert_ids,
        route_weights,
        queries,
        cache,
        resid,
        norm_gain.reshape(1, width),
        uv_weight,
        out_weight,
        gate_weight,
        up_weight,
        down_weight,
    )


def solution(mesh):
    return jax.shard_map(
        on_device,
        mesh=mesh,
        in_specs=(
            P(("group", "ep", "side"), None, None),
            P(("group", "ep", "side"), None, None),
            P(("group", "ep", "side")),
            P(("group", "ep", "side"), None),
            P(("ep", "side"), None, None),
            P(("ep", "side"), None),
            P(),
            P(("group", "ep", "side"), None),
            P(("group", "ep", "side"), None),
            P("ep", None, "side"),
            P("ep", None, "side"),
            P("ep", "side", None),
        ),
        out_specs=P(("group", "ep", "side"), None),
        check_vma=False,
    )
```

```python
import functools

import jax
import jax.numpy as jnp
from jax import lax
from jax.experimental import pallas as pl
from jax.experimental.pallas import tpu as pltpu
from jax.sharding import PartitionSpec as P

F32 = jnp.float32
BF16 = jnp.bfloat16
MESH = pl.DeviceIdType.MESH
CHUNKS = 2


def layer_kernel(
    ep_n,
    side_n,
    lengths,
    ids,
    route,
    q_hbm,
    cache_hbm,
    resid,
    gain,
    uv_hbm,
    ow_hbm,
    gw_hbm,
    uw_hbm,
    dw_hbm,
    out,
    q,
    cache,
    uv,
    ow,
    gw,
    uw,
    dw,
    ctx_tx,
    ctx_rx,
    ctx_rows,
    vals,
    cf_tx,
    cf_rx,
    cf_rows,
    part,
    t1,
    r1,
    t2,
    r2,
    t3,
    r3,
    keep,
    hidden,
    gath,
    xrows,
    in_sem,
    ow_sem,
    gw_sem,
    uw_sem,
    dw_sem,
    ctx_send,
    ctx_recv,
    cf_send,
    cf_recv,
    rs_send,
    rs_recv,
    ag_send,
    ag_recv,
):
    n = ep_n * side_n
    x_n = ep_n // 2
    ep = lax.axis_index("ep")
    side = lax.axis_index("side")
    me = ep * side_n + side
    x = ep // 2
    core = lax.rem(ep, 2)
    rows_here, _, heads = q_hbm.shape
    heads_here, latent, value_size = uv_hbm.shape
    slots = cache_hbm.shape[2]
    width = resid.shape[1]
    piece = width // CHUNKS
    rows = n * rows_here
    block = side_n * rows_here

    def at(group_index):
        return {"ep": group_index // side_n, "side": lax.rem(group_index, side_n)}

    def remote(src, dst, send, recv, device):
        return pltpu.make_async_remote_copy(
            src_ref=src, dst_ref=dst, send_sem=send, recv_sem=recv, device_id=device, device_id_type=MESH
        )

    barrier = pltpu.get_barrier_semaphore()

    @pl.loop(1, n)
    def _(i):
        pl.semaphore_signal(barrier, inc=1, device_id=at(lax.rem(me + i, n)), device_id_type=MESH)

    loads = [
        pltpu.make_async_copy(cache_hbm, cache, in_sem.at[0]),
        pltpu.make_async_copy(q_hbm, q, in_sem.at[1]),
        pltpu.make_async_copy(uv_hbm, uv, in_sem.at[2]),
    ]
    for load in loads:
        load.start()
    cut = [pl.ds(c * piece, piece) for c in range(CHUNKS)]
    ow_load = [pltpu.make_async_copy(ow_hbm.at[:, s], ow.at[:, s], ow_sem.at[c]) for c, s in enumerate(cut)]
    gw_load = [pltpu.make_async_copy(gw_hbm.at[0, s], gw.at[s], gw_sem.at[c]) for c, s in enumerate(cut)]
    uw_load = [pltpu.make_async_copy(uw_hbm.at[0, s], uw.at[s], uw_sem.at[c]) for c, s in enumerate(cut)]
    dw_load = [pltpu.make_async_copy(dw_hbm.at[0, :, s], dw.at[:, s], dw_sem.at[c]) for c, s in enumerate(cut)]
    for load in ow_load:
        load.start()

    lane = lax.broadcasted_iota(jnp.int32, (1, 128), 1)
    for r in range(rows_here):
        line = jnp.zeros((1, 128), F32)
        for k in range(ids.shape[1]):
            line += jnp.where(lane == ids[r, k], route[r, k], 0.0)
        cf_tx[r : r + 1, :] = line
    cf_rx[me] = cf_tx[...]

    def attend(r):
        scores = lax.dot_general(
            q[r], cache[r], (((0,), (0,)), ((), ())), preferred_element_type=F32
        ) * (1.0 / 192.0**0.5)
        valid = lax.broadcasted_iota(jnp.int32, (heads, slots), 1) < lengths[r]
        top = jnp.max(jnp.where(valid, scores, -1e30), axis=1, keepdims=True)
        expo = jnp.where(valid, jnp.exp(scores - top), 0.0)
        probs = (expo / jnp.sum(expo, axis=1, keepdims=True)).astype(BF16)
        context = lax.dot_general(
            probs, cache[r, :latent, :], (((1,), (1,)), ((), ())), preferred_element_type=F32
        )
        for d in range(n):
            ctx_tx[r, d] = context[d * heads_here : (d + 1) * heads_here].astype(BF16)
        ctx_rx[r, me] = ctx_tx[r, me]

    def send_context(r):
        @pl.loop(1, n)
        def _(i):
            there = lax.rem(me + i, n)
            remote(
                ctx_tx.at[r, there], ctx_rx.at[r, me], ctx_send.at[r, i - 1], ctx_recv.at[r, i - 1], at(there)
            ).start()

    loads[0].wait()
    loads[1].wait()
    for r in range(rows_here):
        attend(r)
        if r == 0:
            pl.semaphore_wait(barrier, n - 1)
        send_context(r)

    @pl.loop(1, n)
    def _(i):
        remote(cf_tx, cf_rx.at[me], cf_send.at[i - 1], cf_recv.at[i - 1], at(lax.rem(me + i, n))).start()

    loads[2].wait()
    for r in range(rows_here):

        @pl.loop(1, n)
        def _(i):
            origin = lax.rem(me + n - i, n)
            remote(
                ctx_tx.at[r, origin], ctx_rx.at[r, origin], ctx_send.at[r, i - 1], ctx_recv.at[r, i - 1], at(origin)
            ).wait_recv()

    for c in range(CHUNKS):
        gw_load[c].start()
        uw_load[c].start()
    for load in dw_load:
        load.start()

    for r in range(rows_here):
        for d in range(n):
            first = (d * rows_here + r) * heads_here
            arrived = ctx_rx[r, d].astype(F32)
            for j in range(latent // 128):
                ctx_rows[j, first : first + heads_here] = arrived[:, j * 128 : (j + 1) * 128]
    for h in range(heads_here):
        picked = pl.ds(h, rows, stride=heads_here) if heads_here > 1 else pl.ds(0, rows)
        taken = jnp.concatenate([ctx_rows[j, picked, :] for j in range(latent // 128)], axis=1)
        vals[:, h * value_size : (h + 1) * value_size] = jnp.dot(
            taken.astype(BF16), uv[h], preferred_element_type=F32
        ).astype(BF16)

    def reduce_copies(p, c):
        core_copy = remote(
            t1.at[p, c], r1.at[p, c], rs_send.at[p, c, 0], rs_recv.at[p, c, 0], {"ep": ep + 1 - 2 * core}
        )
        x_copies, side_copies = [], []
        for i in range(1, x_n):
            there = lax.rem(x + i, x_n) * 2 + core
            for s in range(side_n):
                k = 1 + (i - 1) * side_n + s
                x_copies.append(
                    remote(
                        t2.at[p, c, i - 1, s],
                        r2.at[p, c, i - 1, s],
                        rs_send.at[p, c, k],
                        rs_recv.at[p, c, k],
                        {"ep": there},
                    )
                )
        for i in range(1, side_n):
            k = (x_n - 1) * side_n + i
            there = lax.rem(side + i, side_n)
            side_copies.append(
                remote(t3.at[p, c, there], r3.at[p, c, i - 1], rs_send.at[p, c, k], rs_recv.at[p, c, k], {"side": there})
            )
        return core_copy, x_copies, side_copies

    def reduce_scatter(p, product):
        copies = [reduce_copies(p, c) for c in range(CHUNKS)]
        totals = []
        for step in range(CHUNKS + 2):
            c = step
            if c < CHUNKS:
                part[c] = product(c).reshape(ep_n, block, piece)
                for k in range(x_n):
                    t1[p, c, k] = part[c, 2 * k + 1 - core].astype(BF16)
                copies[c][0].start()
            c = step - 1
            if 0 <= c < CHUNKS:
                copies[c][0].wait_recv()
                for i in range(1, x_n):
                    k = lax.rem(x + i, x_n)
                    ahead = (part[c, 2 * k + core] + r1[p, c, k].astype(F32)).astype(BF16)
                    for s in range(side_n):
                        t2[p, c, i - 1, s] = ahead[s * rows_here : (s + 1) * rows_here]
                        copies[c][1][(i - 1) * side_n + s].start()
            c = step - 2
            if 0 <= c < CHUNKS:
                total = part[c, ep] + r1[p, c, x].astype(F32)
                for s in range(side_n):
                    mine = total[s * rows_here : (s + 1) * rows_here]
                    for i in range(1, x_n):
                        copies[c][1][(i - 1) * side_n + s].wait_recv()
                        mine += r2[p, c, i - 1, s].astype(F32)
                    keep[c, s] = mine
                    t3[p, c, s] = mine.astype(BF16)
                    away = lax.rem(s - side + side_n, side_n)

                    @pl.when(away > 0)
                    def _():
                        k = (x_n - 1) * side_n + away
                        remote(
                            t3.at[p, c, s], r3.at[p, c, away - 1], rs_send.at[p, c, k], rs_recv.at[p, c, k], {"side": s}
                        ).start()
        for c in range(CHUNKS):
            total = keep[c, side]
            for i in range(1, side_n):
                copies[c][2][i - 1].wait_recv()
                total += r3[p, c, i - 1].astype(F32)
            totals.append(total)
        return totals, copies

    def out_product(c):
        ow_load[c].wait()
        return jnp.dot(vals[...], ow[:, cut[c]], preferred_element_type=F32)

    attn, copies_a = reduce_scatter(0, out_product)

    square = jnp.zeros((rows_here, 1), F32)
    for c in range(CHUNKS):
        state = (resid[:, cut[c]].astype(F32) + attn[c]).astype(BF16).astype(F32)
        hidden[:, cut[c]] = state
        square += jnp.sum(state * state, axis=1, keepdims=True)
    inverse = lax.rsqrt(square * (1.0 / width) + 1e-06)

    def gather_copies(c):
        def blocks(index):
            return gath.at[c, pl.ds(index * side_n, side_n)]

        side_out, side_in, x_out, x_in, core_out, core_in = [], [], [], [], [], []
        for i in range(1, side_n):
            k = i - 1
            origin = ep * side_n + lax.rem(side + side_n - i, side_n)
            there = {"side": lax.rem(side + i, side_n)}
            side_out.append(remote(gath.at[c, me], gath.at[c, me], ag_send.at[c, k], ag_recv.at[c, k], there))
            side_in.append(remote(gath.at[c, origin], gath.at[c, origin], ag_send.at[c, k], ag_recv.at[c, k], there))
        for i in range(1, x_n):
            origin = lax.rem(x + x_n - i, x_n) * 2 + core
            there = {"ep": lax.rem(x + i, x_n) * 2 + core}
            for j in range(side_n):
                k = side_n - 1 + (i - 1) * side_n + j
                turn = lax.rem(side + side_n - j, side_n)
                mine, other = gath.at[c, ep * side_n + turn], gath.at[c, origin * side_n + turn]
                x_out.append(remote(mine, mine, ag_send.at[c, k], ag_recv.at[c, k], there))
                x_in.append(remote(other, other, ag_send.at[c, k], ag_recv.at[c, k], there))
        for i in range(x_n):
            k = side_n - 1 + (x_n - 1) * side_n + i
            origin = lax.rem(x + x_n - i, x_n) * 2
            sibling = {"ep": ep + 1 - 2 * core}
            mine, other = blocks(origin + core), blocks(origin + 1 - core)
            core_out.append(remote(mine, mine, ag_send.at[c, k], ag_recv.at[c, k], sibling))
            core_in.append(remote(other, other, ag_send.at[c, k], ag_recv.at[c, k], sibling))
        return side_out, side_in, x_out, x_in, core_out, core_in

    gathers = [gather_copies(c) for c in range(CHUNKS)]
    gains = gain[...].astype(F32)
    for c in range(CHUNKS):
        first = c * piece // 128
        gain_row = jnp.concatenate([gains[first + j : first + j + 1] for j in range(piece // 128)], axis=1)
        gath[c, me] = (hidden[:, cut[c]] * inverse * gain_row).astype(BF16)
        for copy in gathers[c][0]:
            copy.start()
        for i in range(1, x_n):
            gathers[c][2][(i - 1) * side_n].start()
    for c in range(CHUNKS):
        for j in range(1, side_n):
            gathers[c][1][j - 1].wait_recv()
            for i in range(1, x_n):
                gathers[c][2][(i - 1) * side_n + j].start()
        gathers[c][4][0].start()
    for c in range(CHUNKS):
        for i in range(1, x_n):
            for j in range(side_n):
                gathers[c][3][(i - 1) * side_n + j].wait_recv()
            gathers[c][4][i].start()

    @pl.loop(1, n)
    def _(i):
        origin = lax.rem(me + n - i, n)
        remote(cf_tx, cf_rx.at[origin], cf_send.at[i - 1], cf_recv.at[i - 1], at(origin)).wait_recv()

    for d in range(n):
        cf_rows[d * rows_here : (d + 1) * rows_here] = cf_rx[d]
    coef = jnp.sum(jnp.where(lane == ep, cf_rows[...], 0.0), axis=1, keepdims=True)

    gate = jnp.zeros((rows, gw.shape[1]), F32)
    upper = jnp.zeros((rows, gw.shape[1]), F32)
    for c in range(CHUNKS):
        for copy in gathers[c][5]:
            copy.wait_recv()
        for d in range(n):
            xrows[c, d * rows_here : (d + 1) * rows_here] = gath[c, d].astype(F32)
        normed = xrows[c].astype(BF16)
        gw_load[c].wait()
        uw_load[c].wait()
        gate += jnp.dot(normed, gw[cut[c]], preferred_element_type=F32)
        upper += jnp.dot(normed, uw[cut[c]], preferred_element_type=F32)
    inner = (jax.nn.silu(gate) * upper * coef).astype(BF16)

    def down_product(c):
        dw_load[c].wait()
        return jnp.dot(inner, dw[:, cut[c]], preferred_element_type=F32)

    mixed, copies_b = reduce_scatter(1, down_product)
    for c in range(CHUNKS):
        out[:, cut[c]] = (hidden[:, cut[c]] + mixed[c]).astype(out.dtype)

    @pl.loop(1, n)
    def _(i):
        there = lax.rem(me + i, n)
        for r in range(rows_here):
            remote(
                ctx_tx.at[r, there], ctx_rx.at[r, me], ctx_send.at[r, i - 1], ctx_recv.at[r, i - 1], at(there)
            ).wait_send()
        remote(cf_tx, cf_rx.at[me], cf_send.at[i - 1], cf_recv.at[i - 1], at(there)).wait_send()

    for copies in (copies_a, copies_b):
        for core_copy, x_copies, side_copies in copies:
            for copy in [core_copy] + x_copies + side_copies:
                copy.wait_send()
    for side_out, _, x_out, _, core_out, _ in gathers:
        for copy in side_out + x_out + core_out:
            copy.wait_send()


def on_device(
    queries,
    cache,
    lengths,
    resid,
    uv_weight,
    out_weight,
    norm_gain,
    expert_ids,
    route_weights,
    gate_weight,
    up_weight,
    down_weight,
):
    ep_n = lax.axis_size("ep")
    side_n = lax.axis_size("side")
    n = ep_n * side_n
    x_n = ep_n // 2
    rows_here, head_count, component_count = queries.shape
    slot_count = cache.shape[1]
    heads_here, latent, value_size = uv_weight.shape
    width = resid.shape[1]
    piece = width // CHUNKS
    rows = n * rows_here
    block = side_n * rows_here
    vmem = pltpu.VMEM
    dma = pltpu.SemaphoreType.DMA
    hops = 1 + (x_n - 1) * side_n + (side_n - 1)
    gather_hops = (side_n - 1) + (x_n - 1) * side_n + x_n
    smem_spec = pl.BlockSpec(memory_space=pltpu.SMEM)
    vmem_spec = pl.BlockSpec(memory_space=pltpu.VMEM)
    any_spec = pl.BlockSpec(memory_space=pl.ANY)
    return pl.pallas_call(
        functools.partial(layer_kernel, ep_n, side_n),
        out_shape=jax.ShapeDtypeStruct(resid.shape, resid.dtype),
        in_specs=[smem_spec] * 3 + [any_spec] * 2 + [vmem_spec] * 2 + [any_spec] * 5,
        out_specs=vmem_spec,
        scratch_shapes=[
            vmem((rows_here, component_count, head_count), BF16),
            vmem((rows_here, component_count, slot_count), BF16),
            vmem(uv_weight.shape, BF16),
            vmem(out_weight.shape, BF16),
            vmem(gate_weight.shape[1:], BF16),
            vmem(up_weight.shape[1:], BF16),
            vmem(down_weight.shape[1:], BF16),
            vmem((rows_here, n, heads_here, latent), BF16),
            vmem((rows_here, n, heads_here, latent), BF16),
            vmem((latent // 128, rows * heads_here, 128), F32),
            vmem((rows, heads_here * value_size), BF16),
            vmem((rows_here, 128), F32),
            vmem((n, rows_here, 128), F32),
            vmem((rows, 128), F32),
            vmem((CHUNKS, ep_n, block, piece), F32),
            vmem((2, CHUNKS, x_n, block, piece), BF16),
            vmem((2, CHUNKS, x_n, block, piece), BF16),
            vmem((2, CHUNKS, x_n - 1, side_n, rows_here, piece), BF16),
            vmem((2, CHUNKS, x_n - 1, side_n, rows_here, piece), BF16),
            vmem((2, CHUNKS, side_n, rows_here, piece), BF16),
            vmem((2, CHUNKS, side_n - 1, rows_here, piece), BF16),
            vmem((CHUNKS, side_n, rows_here, piece), F32),
            vmem((rows_here, width), F32),
            vmem((CHUNKS, n, rows_here, piece), BF16),
            vmem((CHUNKS, rows, piece), F32),
            dma((3,)),
            dma((CHUNKS,)),
            dma((CHUNKS,)),
            dma((CHUNKS,)),
            dma((CHUNKS,)),
            dma((rows_here, n - 1)),
            dma((rows_here, n - 1)),
            dma((n - 1,)),
            dma((n - 1,)),
            dma((2, CHUNKS, hops)),
            dma((2, CHUNKS, hops)),
            dma((CHUNKS, gather_hops)),
            dma((CHUNKS, gather_hops)),
        ],
        compiler_params=pltpu.CompilerParams(
            collective_id=0, has_side_effects=True, vmem_limit_bytes=56 * 2**20
        ),
    )(
        lengths,
        expert_ids,
        route_weights,
        jnp.swapaxes(queries, 1, 2),
        jnp.swapaxes(cache, 1, 2),
        resid,
        norm_gain.reshape(width // 128, 128),
        uv_weight,
        out_weight,
        gate_weight,
        up_weight,
        down_weight,
    )


def solution(mesh):
    return jax.shard_map(
        on_device,
        mesh=mesh,
        in_specs=(
            P(("group", "ep", "side"), None, None),
            P(("group", "ep", "side"), None, None),
            P(("group", "ep", "side")),
            P(("group", "ep", "side"), None),
            P(("ep", "side"), None, None),
            P(("ep", "side"), None),
            P(),
            P(("group", "ep", "side"), None),
            P(("group", "ep", "side"), None),
            P("ep", None, "side"),
            P("ep", None, "side"),
            P("ep", "side", None),
        ),
        out_specs=P(("group", "ep", "side"), None),
        check_vma=False,
    )
```

```python
import functools

import jax
import jax.numpy as jnp
from jax import lax
from jax.experimental import pallas as pl
from jax.experimental.pallas import tpu as pltpu
from jax.sharding import PartitionSpec as P

F32 = jnp.float32
BF16 = jnp.bfloat16
MESH = pl.DeviceIdType.MESH
CHUNKS = 2


def layer_kernel(
    ep_n,
    side_n,
    lengths,
    ids,
    route,
    q_hbm,
    cache_hbm,
    resid,
    gain,
    uv_hbm,
    ow_hbm,
    gw_hbm,
    uw_hbm,
    dw_hbm,
    out,
    q,
    cache,
    uv,
    ow,
    gw,
    uw,
    dw,
    ctx_tx,
    ctx_rx,
    ctx_rows,
    vals,
    cf_tx,
    cf_rx,
    cf_rows,
    part,
    t1,
    r1,
    t2,
    r2,
    t3,
    r3,
    keep,
    hidden,
    gath,
    xrows,
    in_sem,
    ow_sem,
    gw_sem,
    uw_sem,
    dw_sem,
    ctx_send,
    ctx_recv,
    cf_send,
    cf_recv,
    rs_send,
    rs_recv,
    ag_send,
    ag_recv,
):
    n = ep_n * side_n
    x_n = ep_n // 2
    ep = lax.axis_index("ep")
    side = lax.axis_index("side")
    me = ep * side_n + side
    x = ep // 2
    core = lax.rem(ep, 2)
    rows_here, _, heads = q_hbm.shape
    heads_here, latent, value_size = uv_hbm.shape
    slots = cache_hbm.shape[2]
    width = resid.shape[1]
    piece = width // CHUNKS
    rows = n * rows_here
    block = side_n * rows_here

    def at(group_index):
        return {"ep": group_index // side_n, "side": lax.rem(group_index, side_n)}

    def remote(src, dst, send, recv, device):
        return pltpu.make_async_remote_copy(
            src_ref=src, dst_ref=dst, send_sem=send, recv_sem=recv, device_id=device, device_id_type=MESH
        )

    barrier = pltpu.get_barrier_semaphore()

    @pl.loop(1, n)
    def _(i):
        pl.semaphore_signal(barrier, inc=1, device_id=at(lax.rem(me + i, n)), device_id_type=MESH)

    loads = [
        pltpu.make_async_copy(cache_hbm, cache, in_sem.at[0]),
        pltpu.make_async_copy(q_hbm, q, in_sem.at[1]),
        pltpu.make_async_copy(uv_hbm, uv, in_sem.at[2]),
    ]
    for load in loads:
        load.start()
    cut = [pl.ds(c * piece, piece) for c in range(CHUNKS)]
    ow_load = [pltpu.make_async_copy(ow_hbm.at[:, s], ow.at[:, s], ow_sem.at[c]) for c, s in enumerate(cut)]
    gw_load = [pltpu.make_async_copy(gw_hbm.at[0, s], gw.at[s], gw_sem.at[c]) for c, s in enumerate(cut)]
    uw_load = [pltpu.make_async_copy(uw_hbm.at[0, s], uw.at[s], uw_sem.at[c]) for c, s in enumerate(cut)]
    dw_load = [pltpu.make_async_copy(dw_hbm.at[0, :, s], dw.at[:, s], dw_sem.at[c]) for c, s in enumerate(cut)]
    for load in ow_load:
        load.start()

    lane = lax.broadcasted_iota(jnp.int32, (1, 128), 1)
    for r in range(rows_here):
        line = jnp.zeros((1, 128), F32)
        for k in range(ids.shape[1]):
            line += jnp.where(lane == ids[r, k], route[r, k], 0.0)
        cf_tx[r : r + 1, :] = line
    cf_rx[me] = cf_tx[...]

    def attend(r):
        scores = lax.dot_general(
            q[r], cache[r], (((0,), (0,)), ((), ())), preferred_element_type=F32
        ) * (1.0 / 192.0**0.5)
        valid = lax.broadcasted_iota(jnp.int32, (heads, slots), 1) < lengths[r]
        top = jnp.max(jnp.where(valid, scores, -1e30), axis=1, keepdims=True)
        expo = jnp.where(valid, jnp.exp(scores - top), 0.0)
        probs = (expo / jnp.sum(expo, axis=1, keepdims=True)).astype(BF16)
        context = lax.dot_general(
            probs, cache[r, :latent, :], (((1,), (1,)), ((), ())), preferred_element_type=F32
        )
        for d in range(n):
            ctx_tx[d, r] = context[d * heads_here : (d + 1) * heads_here].astype(BF16)
        ctx_rx[me, r] = ctx_tx[me, r]

    def context_copy(i, source, target, there):
        return remote(ctx_tx.at[source], ctx_rx.at[target], ctx_send.at[i - 1], ctx_recv.at[i - 1], at(there))

    loads[0].wait()
    loads[1].wait()
    for r in range(rows_here):
        attend(r)
    pl.semaphore_wait(barrier, n - 1)

    @pl.loop(1, n)
    def _(i):
        there = lax.rem(me + i, n)
        context_copy(i, there, me, there).start()

    @pl.loop(1, n)
    def _(i):
        remote(cf_tx, cf_rx.at[me], cf_send.at[i - 1], cf_recv.at[i - 1], at(lax.rem(me + i, n))).start()

    loads[2].wait()

    @pl.loop(1, n)
    def _(i):
        origin = lax.rem(me + n - i, n)
        context_copy(i, origin, origin, origin).wait_recv()

    for c in range(CHUNKS):
        gw_load[c].start()
        uw_load[c].start()
    for load in dw_load:
        load.start()

    for r in range(rows_here):
        for d in range(n):
            first = (d * rows_here + r) * heads_here
            arrived = ctx_rx[d, r].astype(F32)
            for j in range(latent // 128):
                ctx_rows[j, first : first + heads_here] = arrived[:, j * 128 : (j + 1) * 128]
    for h in range(heads_here):
        picked = pl.ds(h, rows, stride=heads_here) if heads_here > 1 else pl.ds(0, rows)
        taken = jnp.concatenate([ctx_rows[j, picked, :] for j in range(latent // 128)], axis=1)
        vals[:, h * value_size : (h + 1) * value_size] = jnp.dot(
            taken.astype(BF16), uv[h], preferred_element_type=F32
        ).astype(BF16)

    def reduce_copies(p, c):
        core_copy = remote(
            t1.at[p, c], r1.at[p, c], rs_send.at[p, c, 0], rs_recv.at[p, c, 0], {"ep": ep + 1 - 2 * core}
        )
        x_copies, side_copies = [], []
        for i in range(1, x_n):
            there = lax.rem(x + i, x_n) * 2 + core
            for s in range(side_n):
                k = 1 + (i - 1) * side_n + s
                x_copies.append(
                    remote(
                        t2.at[p, c, i - 1, s],
                        r2.at[p, c, i - 1, s],
                        rs_send.at[p, c, k],
                        rs_recv.at[p, c, k],
                        {"ep": there},
                    )
                )
        for i in range(1, side_n):
            k = (x_n - 1) * side_n + i
            there = lax.rem(side + i, side_n)
            side_copies.append(
                remote(t3.at[p, c, there], r3.at[p, c, i - 1], rs_send.at[p, c, k], rs_recv.at[p, c, k], {"side": there})
            )
        return core_copy, x_copies, side_copies

    def reduce_scatter(p, product):
        copies = [reduce_copies(p, c) for c in range(CHUNKS)]
        totals = []
        for step in range(CHUNKS + 2):
            c = step
            if c < CHUNKS:
                part[c] = product(c).reshape(ep_n, block, piece)
                for k in range(x_n):
                    t1[p, c, k] = part[c, 2 * k + 1 - core].astype(BF16)
                copies[c][0].start()
            c = step - 1
            if 0 <= c < CHUNKS:
                copies[c][0].wait_recv()
                for i in range(1, x_n):
                    k = lax.rem(x + i, x_n)
                    ahead = (part[c, 2 * k + core] + r1[p, c, k].astype(F32)).astype(BF16)
                    for s in range(side_n):
                        t2[p, c, i - 1, s] = ahead[s * rows_here : (s + 1) * rows_here]
                        copies[c][1][(i - 1) * side_n + s].start()
            c = step - 2
            if 0 <= c < CHUNKS:
                total = part[c, ep] + r1[p, c, x].astype(F32)
                for s in range(side_n):
                    mine = total[s * rows_here : (s + 1) * rows_here]
                    for i in range(1, x_n):
                        copies[c][1][(i - 1) * side_n + s].wait_recv()
                        mine += r2[p, c, i - 1, s].astype(F32)
                    keep[c, s] = mine
                    t3[p, c, s] = mine.astype(BF16)
                    away = lax.rem(s - side + side_n, side_n)

                    @pl.when(away > 0)
                    def _():
                        k = (x_n - 1) * side_n + away
                        remote(
                            t3.at[p, c, s], r3.at[p, c, away - 1], rs_send.at[p, c, k], rs_recv.at[p, c, k], {"side": s}
                        ).start()
        for c in range(CHUNKS):
            total = keep[c, side]
            for i in range(1, side_n):
                copies[c][2][i - 1].wait_recv()
                total += r3[p, c, i - 1].astype(F32)
            totals.append(total)
        return totals, copies

    def out_product(c):
        ow_load[c].wait()
        return jnp.dot(vals[...], ow[:, cut[c]], preferred_element_type=F32)

    attn, copies_a = reduce_scatter(0, out_product)

    square = jnp.zeros((rows_here, 1), F32)
    for c in range(CHUNKS):
        state = (resid[:, cut[c]].astype(F32) + attn[c]).astype(BF16).astype(F32)
        hidden[:, cut[c]] = state
        square += jnp.sum(state * state, axis=1, keepdims=True)
    inverse = lax.rsqrt(square * (1.0 / width) + 1e-06)

    def gather_copies(c):
        def blocks(index):
            return gath.at[c, pl.ds(index * side_n, side_n)]

        side_out, side_in, x_out, x_in, core_out, core_in = [], [], [], [], [], []
        for i in range(1, side_n):
            k = i - 1
            origin = ep * side_n + lax.rem(side + side_n - i, side_n)
            there = {"side": lax.rem(side + i, side_n)}
            side_out.append(remote(gath.at[c, me], gath.at[c, me], ag_send.at[c, k], ag_recv.at[c, k], there))
            side_in.append(remote(gath.at[c, origin], gath.at[c, origin], ag_send.at[c, k], ag_recv.at[c, k], there))
        for i in range(1, x_n):
            origin = lax.rem(x + x_n - i, x_n) * 2 + core
            there = {"ep": lax.rem(x + i, x_n) * 2 + core}
            for j in range(side_n):
                k = side_n - 1 + (i - 1) * side_n + j
                turn = lax.rem(side + side_n - j, side_n)
                mine, other = gath.at[c, ep * side_n + turn], gath.at[c, origin * side_n + turn]
                x_out.append(remote(mine, mine, ag_send.at[c, k], ag_recv.at[c, k], there))
                x_in.append(remote(other, other, ag_send.at[c, k], ag_recv.at[c, k], there))
        for i in range(x_n):
            k = side_n - 1 + (x_n - 1) * side_n + i
            origin = lax.rem(x + x_n - i, x_n) * 2
            sibling = {"ep": ep + 1 - 2 * core}
            mine, other = blocks(origin + core), blocks(origin + 1 - core)
            core_out.append(remote(mine, mine, ag_send.at[c, k], ag_recv.at[c, k], sibling))
            core_in.append(remote(other, other, ag_send.at[c, k], ag_recv.at[c, k], sibling))
        return side_out, side_in, x_out, x_in, core_out, core_in

    gathers = [gather_copies(c) for c in range(CHUNKS)]
    gains = gain[...].astype(F32)
    for c in range(CHUNKS):
        first = c * piece // 128
        gain_row = jnp.concatenate([gains[first + j : first + j + 1] for j in range(piece // 128)], axis=1)
        gath[c, me] = (hidden[:, cut[c]] * inverse * gain_row).astype(BF16)
        for copy in gathers[c][0]:
            copy.start()
        for i in range(1, x_n):
            gathers[c][2][(i - 1) * side_n].start()
    for c in range(CHUNKS):
        for j in range(1, side_n):
            gathers[c][1][j - 1].wait_recv()
            for i in range(1, x_n):
                gathers[c][2][(i - 1) * side_n + j].start()
        gathers[c][4][0].start()
    for c in range(CHUNKS):
        for i in range(1, x_n):
            for j in range(side_n):
                gathers[c][3][(i - 1) * side_n + j].wait_recv()
            gathers[c][4][i].start()

    @pl.loop(1, n)
    def _(i):
        origin = lax.rem(me + n - i, n)
        remote(cf_tx, cf_rx.at[origin], cf_send.at[i - 1], cf_recv.at[i - 1], at(origin)).wait_recv()

    for d in range(n):
        cf_rows[d * rows_here : (d + 1) * rows_here] = cf_rx[d]
    coef = jnp.sum(jnp.where(lane == ep, cf_rows[...], 0.0), axis=1, keepdims=True)

    gate = jnp.zeros((rows, gw.shape[1]), F32)
    upper = jnp.zeros((rows, gw.shape[1]), F32)
    for c in range(CHUNKS):
        for copy in gathers[c][5]:
            copy.wait_recv()
        for d in range(n):
            xrows[c, d * rows_here : (d + 1) * rows_here] = gath[c, d].astype(F32)
        normed = xrows[c].astype(BF16)
        gw_load[c].wait()
        uw_load[c].wait()
        gate += jnp.dot(normed, gw[cut[c]], preferred_element_type=F32)
        upper += jnp.dot(normed, uw[cut[c]], preferred_element_type=F32)
    inner = (jax.nn.silu(gate) * upper * coef).astype(BF16)

    def down_product(c):
        dw_load[c].wait()
        return jnp.dot(inner, dw[:, cut[c]], preferred_element_type=F32)

    mixed, copies_b = reduce_scatter(1, down_product)
    for c in range(CHUNKS):
        out[:, cut[c]] = (hidden[:, cut[c]] + mixed[c]).astype(out.dtype)

    @pl.loop(1, n)
    def _(i):
        there = lax.rem(me + i, n)
        context_copy(i, there, me, there).wait_send()
        remote(cf_tx, cf_rx.at[me], cf_send.at[i - 1], cf_recv.at[i - 1], at(there)).wait_send()

    for copies in (copies_a, copies_b):
        for core_copy, x_copies, side_copies in copies:
            for copy in [core_copy] + x_copies + side_copies:
                copy.wait_send()
    for side_out, _, x_out, _, core_out, _ in gathers:
        for copy in side_out + x_out + core_out:
            copy.wait_send()


def on_device(
    queries,
    cache,
    lengths,
    resid,
    uv_weight,
    out_weight,
    norm_gain,
    expert_ids,
    route_weights,
    gate_weight,
    up_weight,
    down_weight,
):
    ep_n = lax.axis_size("ep")
    side_n = lax.axis_size("side")
    n = ep_n * side_n
    x_n = ep_n // 2
    rows_here, head_count, component_count = queries.shape
    slot_count = cache.shape[1]
    heads_here, latent, value_size = uv_weight.shape
    width = resid.shape[1]
    piece = width // CHUNKS
    rows = n * rows_here
    block = side_n * rows_here
    vmem = pltpu.VMEM
    dma = pltpu.SemaphoreType.DMA
    hops = 1 + (x_n - 1) * side_n + (side_n - 1)
    gather_hops = (side_n - 1) + (x_n - 1) * side_n + x_n
    smem_spec = pl.BlockSpec(memory_space=pltpu.SMEM)
    vmem_spec = pl.BlockSpec(memory_space=pltpu.VMEM)
    any_spec = pl.BlockSpec(memory_space=pl.ANY)
    return pl.pallas_call(
        functools.partial(layer_kernel, ep_n, side_n),
        out_shape=jax.ShapeDtypeStruct(resid.shape, resid.dtype),
        in_specs=[smem_spec] * 3 + [any_spec] * 2 + [vmem_spec] * 2 + [any_spec] * 5,
        out_specs=vmem_spec,
        scratch_shapes=[
            vmem((rows_here, component_count, head_count), BF16),
            vmem((rows_here, component_count, slot_count), BF16),
            vmem(uv_weight.shape, BF16),
            vmem(out_weight.shape, BF16),
            vmem(gate_weight.shape[1:], BF16),
            vmem(up_weight.shape[1:], BF16),
            vmem(down_weight.shape[1:], BF16),
            vmem((n, rows_here, heads_here, latent), BF16),
            vmem((n, rows_here, heads_here, latent), BF16),
            vmem((latent // 128, rows * heads_here, 128), F32),
            vmem((rows, heads_here * value_size), BF16),
            vmem((rows_here, 128), F32),
            vmem((n, rows_here, 128), F32),
            vmem((rows, 128), F32),
            vmem((CHUNKS, ep_n, block, piece), F32),
            vmem((2, CHUNKS, x_n, block, piece), BF16),
            vmem((2, CHUNKS, x_n, block, piece), BF16),
            vmem((2, CHUNKS, x_n - 1, side_n, rows_here, piece), BF16),
            vmem((2, CHUNKS, x_n - 1, side_n, rows_here, piece), BF16),
            vmem((2, CHUNKS, side_n, rows_here, piece), BF16),
            vmem((2, CHUNKS, side_n - 1, rows_here, piece), BF16),
            vmem((CHUNKS, side_n, rows_here, piece), F32),
            vmem((rows_here, width), F32),
            vmem((CHUNKS, n, rows_here, piece), BF16),
            vmem((CHUNKS, rows, piece), F32),
            dma((3,)),
            dma((CHUNKS,)),
            dma((CHUNKS,)),
            dma((CHUNKS,)),
            dma((CHUNKS,)),
            dma((n - 1,)),
            dma((n - 1,)),
            dma((n - 1,)),
            dma((n - 1,)),
            dma((2, CHUNKS, hops)),
            dma((2, CHUNKS, hops)),
            dma((CHUNKS, gather_hops)),
            dma((CHUNKS, gather_hops)),
        ],
        compiler_params=pltpu.CompilerParams(
            collective_id=0, has_side_effects=True, vmem_limit_bytes=56 * 2**20
        ),
    )(
        lengths,
        expert_ids,
        route_weights,
        jnp.swapaxes(queries, 1, 2),
        jnp.swapaxes(cache, 1, 2),
        resid,
        norm_gain.reshape(width // 128, 128),
        uv_weight,
        out_weight,
        gate_weight,
        up_weight,
        down_weight,
    )


def solution(mesh):
    return jax.shard_map(
        on_device,
        mesh=mesh,
        in_specs=(
            P(("group", "ep", "side"), None, None),
            P(("group", "ep", "side"), None, None),
            P(("group", "ep", "side")),
            P(("group", "ep", "side"), None),
            P(("ep", "side"), None, None),
            P(("ep", "side"), None),
            P(),
            P(("group", "ep", "side"), None),
            P(("group", "ep", "side"), None),
            P("ep", None, "side"),
            P("ep", None, "side"),
            P("ep", "side", None),
        ),
        out_specs=P(("group", "ep", "side"), None),
        check_vma=False,
    )
```
